32 devices in a mesh: tile: 8 (over y, x, core), head: 4 (over z).
Axes of the slice: x: 2, y: 2, z: 4, core: 2. Of those that a mesh axis runs over, the one named last changes fastest.
Arguments:
- bott: bfloat16 [16, 128, 1024], P('tile', 'head'), may hold values from -10 to 10
- norm_gain: float32 [1024], replicated, may hold values from 0.1 to 1.9
- w_qkv: bfloat16 [3, 1024, 1024], P(None, None, 'head'), may hold values from -1 to 1
- w_out: bfloat16 [1024, 1024], P('head'), may hold values from -3 to 3
- dw_weight: float32 [3, 3, 1024], replicated, may hold values from -2 to 2
- join_bias: float32 [1024], replicated, may hold values from -3 to 3
- w_join: bfloat16 [1024, 1024], replicated, may hold values from -0.1875 to 0.1875
Outputs:
- joined: bfloat16 [16, 128, 1024], P('tile', 'head')
The draws below stay inside these ranges and needn't reach their ends.
All inputs are finite; a program needn't handle non-finite values.
Results may differ from the reference program's by a relative error of at most 0.02.
Values may be sent and summed in bfloat16 or wider, within the bound.
A program may use at most 128 MiB of HBM per device.

```python
import jax
import jax.numpy as jnp
from jax import lax

D = 1024
HEADS = 16
COLS = 128
SIDE = 16
SEQ = 2048


def draw_bott(key, part):
    return jnp.clip(jax.random.normal(jax.random.fold_in(key, 5), (SIDE, COLS, D), jnp.float32), -6.0, 6.0).astype(jnp.bfloat16)


def draw_w_qkv(key, part):
    factor = D ** (-0.5)
    return (jnp.clip(jax.random.normal(jax.random.fold_in(key, 13), (3, D, D), jnp.float32), -6.0, 6.0) * factor).astype(jnp.bfloat16)


def level_of(stream_key, shape, pieces, low, high):
    def one(dim, shards_of):
        steps = jax.random.uniform(jax.random.fold_in(jax.random.fold_in(stream_key, 6), dim), (shards_of,), jnp.float32, low / len(pieces), high / len(pieces))
        return jnp.repeat(jnp.exp(steps), shape[dim] // shards_of).reshape((-1,) + (1,) * (len(shape) - dim - 1))

    gain = one(*pieces[0])
    for cut in pieces[1:]:
        gain = gain * one(*cut)
    return gain


def bell_draw(own_key, extent, width, limit, pieces=(), dtype=jnp.bfloat16):
    entries = width * jax.random.normal(own_key, extent, jnp.float32)
    if pieces:
        entries = entries * level_of(own_key, extent, pieces, -0.22, 0.18)
    return jnp.clip(entries, -limit, limit).astype(dtype)


def setup_inputs(seed: int = 0) -> dict:
    seeds = jax.random.split(jax.random.key(seed), 8)
    return {
        "bott": draw_bott(jax.random.fold_in(seeds[7], 71), 0),
        "norm_gain": jnp.clip(1.0 + 0.18 * jax.random.normal(seeds[1], (D,), jnp.float32), 0.1, 1.9),
        "w_qkv": draw_w_qkv(jax.random.fold_in(seeds[7], 71), 0),
        "w_out": bell_draw(seeds[3], (D, D), (24.0 / D ** 0.5), 3.0, ((0, 4),)),
        "dw_weight": bell_draw(seeds[4], (3, 3, D), 9 ** -0.5, 2.0, (), jnp.float32),
        "join_bias": bell_draw(seeds[5], (D,), 0.5, 3.0, (), jnp.float32),
        "w_join": bell_draw(seeds[6], (D, D), D ** -0.5, 0.1875),
    }


def reference(bott, norm_gain, w_qkv, w_out, dw_weight, join_bias, w_join):
    values = bott.astype(jnp.float32)
    normed = (values * lax.rsqrt(lax.optimization_barrier(jnp.mean(values * values, axis=-1, keepdims=True)) + 1e-06) * norm_gain).astype(jnp.bfloat16)
    flat = normed.reshape(SEQ, D)
    query = jnp.dot(flat, w_qkv[0], preferred_element_type=jnp.float32).astype(jnp.bfloat16)
    keys = jnp.dot(flat, w_qkv[1], preferred_element_type=jnp.float32).astype(jnp.bfloat16)
    vals = jnp.dot(flat, w_qkv[2], preferred_element_type=jnp.float32).astype(jnp.bfloat16)
    head_dim = D // HEADS
    scale = 1.0 / head_dim ** 0.5
    query_heads = jnp.transpose(query.reshape(SEQ, HEADS, head_dim), (1, 0, 2))
    key_heads = jnp.transpose(keys.reshape(SEQ, HEADS, head_dim), (1, 0, 2))
    value_heads = jnp.transpose(vals.reshape(SEQ, HEADS, head_dim), (1, 0, 2))
    block = min(SEQ, 1024)

    def one_head(args):
        query_h, key_h, value_h = args
        blocks = query_h.reshape(SEQ // block, block, head_dim)

        def one_block(query_block):
            scores = jnp.dot(query_block.astype(jnp.float32), key_h.astype(jnp.float32).T) * scale
            top = lax.optimization_barrier(jnp.max(scores, axis=-1, keepdims=True))
            weights = jnp.exp(scores - top)
            total = lax.optimization_barrier(jnp.sum(weights, axis=-1, keepdims=True))
            summed = jnp.dot(weights.astype(jnp.bfloat16), value_h, preferred_element_type=jnp.float32)
            return (summed / total).astype(jnp.bfloat16)
        return lax.map(one_block, blocks).reshape(SEQ, head_dim)
    attended = lax.map(one_head, (query_heads, key_heads, value_heads))
    attended = jnp.transpose(attended, (1, 0, 2)).reshape(SEQ, D)
    mixed = jnp.dot(attended, w_out, preferred_element_type=jnp.float32)
    context = (values.reshape(SEQ, D) + mixed).astype(jnp.bfloat16).reshape(SIDE, COLS, D)
    padded = jnp.pad(context.astype(jnp.float32), ((1, 1), (1, 1), (0, 0)))
    conv = jnp.zeros((SIDE, COLS, D), jnp.float32)
    for i in range(3):
        for j in range(3):
            conv = conv + padded[i:i + SIDE, j:j + COLS] * dw_weight[i, j]
    hidden = jax.nn.gelu(conv + join_bias).astype(jnp.bfloat16)
    projected = jnp.dot(hidden.reshape(SEQ, D), w_join, preferred_element_type=jnp.float32).reshape(SIDE, COLS, D)
    return (context.astype(jnp.float32) + projected).astype(jnp.bfloat16)
```

```python
import math

import jax
import jax.numpy as jnp
from jax import lax
from jax.sharding import PartitionSpec as P

HEADS = 16


def with_halo(x, sides, width):
    for axis, dim in sides:
        size, length = (lax.axis_size(axis), x.shape[dim])
        up = [(i, (i + 1) % size) for i in range(size - 1)]
        down = [(j, i) for i, j in up]
        last = lax.slice_in_dim(x, length - width, length, axis=dim)
        leading = lax.slice_in_dim(x, 0, width, axis=dim)
        before = lax.ppermute(last, axis, up)
        after = lax.ppermute(leading, axis, down)
        x = jnp.concatenate([before, x, after], axis=dim)
    return x


def fold_blocks(state, queries, key_piece, value_piece, scale):
    count, heads_here, head_dim = key_piece.shape
    block = math.gcd(count, 2048)
    key_blocks = key_piece.reshape(count // block, block, heads_here, head_dim)
    value_blocks = value_piece.reshape(count // block, block, heads_here, head_dim)

    def one_block(inner, pair):
        maxes, totals, summed = inner
        key_block, value_block = pair
        scores = (
            jnp.einsum("qhe,khe->hqk", queries, key_block, preferred_element_type=jnp.float32)
            * scale
        )
        new_max = jnp.maximum(maxes, jnp.max(scores, axis=-1))
        weights = jnp.exp(scores - new_max[..., None])
        decay = jnp.exp(maxes - new_max)
        totals = totals * decay + jnp.sum(weights, axis=-1)
        summed = summed * decay[..., None] + jnp.einsum(
            "hqk,khe->hqe",
            weights.astype(jnp.bfloat16),
            value_block,
            preferred_element_type=jnp.float32,
        )
        return ((new_max, totals, summed), None)

    return lax.scan(one_block, state, (key_blocks, value_blocks))[0]


def empty_state(heads_here, query_count, head_dim):
    return (
        jnp.full((heads_here, query_count), -1e30, jnp.float32),
        jnp.zeros((heads_here, query_count), jnp.float32),
        jnp.zeros((heads_here, query_count, head_dim), jnp.float32),
    )


def per_device(bott, norm_gain, w_qkv, w_out, dw_weight, join_bias, w_join):
    rows, cols_dev, width = bott.shape
    values = bott.astype(jnp.float32)
    normed = (
        values * lax.rsqrt(jnp.mean(values * values, axis=-1, keepdims=True) + 1e-06) * norm_gain
    ).astype(jnp.bfloat16)
    gathered = lax.all_gather(normed, "head", axis=1, tiled=True)
    columns = gathered.shape[1]
    local_width = w_qkv.shape[2]
    head_dim = width // HEADS
    local_heads = local_width // head_dim
    seq_local = columns * rows
    scale = 1.0 / head_dim**0.5
    tokens = jnp.transpose(gathered, (1, 0, 2)).reshape(seq_local, width)
    projected = jnp.einsum(
        "td,jde->jte", tokens, w_qkv, preferred_element_type=jnp.float32
    ).astype(jnp.bfloat16)
    queries = projected[0].reshape(seq_local, local_heads, head_dim)
    keys = projected[1]
    vals = projected[2]
    start_state = empty_state(local_heads, seq_local, head_dim)
    key_piece = lax.all_gather(keys, "tile", axis=0, tiled=True)
    value_piece = lax.all_gather(vals, "tile", axis=0, tiled=True)
    count = key_piece.shape[0]
    maxes, totals, summed = fold_blocks(
        start_state,
        queries,
        key_piece.reshape(count, local_heads, head_dim),
        value_piece.reshape(count, local_heads, head_dim),
        scale,
    )
    attended = (summed / totals[..., None]).astype(jnp.bfloat16)
    attended = jnp.transpose(attended, (1, 0, 2)).reshape(columns, rows, local_width)
    mixed = lax.psum_scatter(
        jnp.einsum("crh,hd->crd", attended, w_out, preferred_element_type=jnp.float32).astype(
            jnp.bfloat16
        ),
        "head",
        scatter_dimension=0,
        tiled=True,
    ).astype(jnp.float32)
    context = (values + jnp.transpose(mixed, (1, 0, 2))).astype(jnp.bfloat16)
    padded = with_halo(context, (("tile", 0), ("head", 1)), 1).astype(jnp.float32)
    conv = jnp.zeros((rows, cols_dev, width), jnp.float32)
    for i in range(3):
        for j in range(3):
            conv = conv + padded[i : i + rows, j : j + cols_dev] * dw_weight[i, j]
    hidden = jax.nn.gelu(conv + join_bias).astype(jnp.bfloat16)
    projected_out = jnp.einsum("rcd,de->rce", hidden, w_join, preferred_element_type=jnp.float32)
    return (context.astype(jnp.float32) + projected_out).astype(jnp.bfloat16)


def solution(mesh):
    placed = (P("tile", "head", None), P(), P(None, None, "head"), P("head", None), P(), P(), P())
    return jax.shard_map(
        per_device, mesh=mesh, in_specs=placed, out_specs=P("tile", "head", None), check_vma=False
    )
```

```python
import functools
import math

import jax
import jax.numpy as jnp
from jax import lax
from jax.experimental import pallas as pl
from jax.experimental.pallas import tpu as pltpu
from jax.sharding import PartitionSpec as P

HEADS = 16


def with_halo(x, sides, width):
    for axis, dim in sides:
        size, length = (lax.axis_size(axis), x.shape[dim])
        up = [(i, (i + 1) % size) for i in range(size - 1)]
        down = [(j, i) for i, j in up]
        last = lax.slice_in_dim(x, length - width, length, axis=dim)
        leading = lax.slice_in_dim(x, 0, width, axis=dim)
        before = lax.ppermute(last, axis, up)
        after = lax.ppermute(leading, axis, down)
        x = jnp.concatenate([before, x, after], axis=dim)
    return x


def fold_blocks(state, queries, key_piece, value_piece, scale):
    count, heads_here, head_dim = key_piece.shape
    block = math.gcd(count, 2048)
    key_blocks = key_piece.reshape(count // block, block, heads_here, head_dim)
    value_blocks = value_piece.reshape(count // block, block, heads_here, head_dim)

    def one_block(inner, pair):
        maxes, totals, summed = inner
        key_block, value_block = pair
        scores = (
            jnp.einsum("qhe,khe->hqk", queries, key_block, preferred_element_type=jnp.float32)
            * scale
        )
        new_max = jnp.maximum(maxes, jnp.max(scores, axis=-1))
        weights = jnp.exp(scores - new_max[..., None])
        decay = jnp.exp(maxes - new_max)
        totals = totals * decay + jnp.sum(weights, axis=-1)
        summed = summed * decay[..., None] + jnp.einsum(
            "hqk,khe->hqe",
            weights.astype(jnp.bfloat16),
            value_block,
            preferred_element_type=jnp.float32,
        )
        return ((new_max, totals, summed), None)

    return lax.scan(one_block, state, (key_blocks, value_blocks))[0]


def empty_state(heads_here, query_count, head_dim):
    return (
        jnp.full((heads_here, query_count), -1e30, jnp.float32),
        jnp.zeros((heads_here, query_count), jnp.float32),
        jnp.zeros((heads_here, query_count, head_dim), jnp.float32),
    )


def per_device(bott, norm_gain, w_qkv, w_out, dw_weight, join_bias, w_join):
    rows, cols_dev, width = bott.shape
    values = bott.astype(jnp.float32)
    normed = (
        values * lax.rsqrt(jnp.mean(values * values, axis=-1, keepdims=True) + 1e-06) * norm_gain
    ).astype(jnp.bfloat16)
    gathered = lax.all_gather(normed, "head", axis=1, tiled=True)
    columns = gathered.shape[1]
    local_width = w_qkv.shape[2]
    head_dim = width // HEADS
    local_heads = local_width // head_dim
    seq_local = columns * rows
    scale = 1.0 / head_dim**0.5
    tokens = jnp.transpose(gathered, (1, 0, 2)).reshape(seq_local, width)
    projected = jnp.einsum(
        "td,jde->jte", tokens, w_qkv, preferred_element_type=jnp.float32
    ).astype(jnp.bfloat16)
    queries = projected[0].reshape(seq_local, local_heads, head_dim)
    keys = projected[1]
    vals = projected[2]
    start_state = empty_state(local_heads, seq_local, head_dim)
    key_piece = lax.all_gather(keys, "tile", axis=0, tiled=True)
    value_piece = lax.all_gather(vals, "tile", axis=0, tiled=True)
    count = key_piece.shape[0]
    maxes, totals, summed = fold_blocks(
        start_state,
        queries,
        key_piece.reshape(count, local_heads, head_dim),
        value_piece.reshape(count, local_heads, head_dim),
        scale,
    )
    attended = (summed / totals[..., None]).astype(jnp.bfloat16)
    attended = jnp.transpose(attended, (1, 0, 2)).reshape(columns, rows, local_width)
    mixed = lax.psum_scatter(
        jnp.einsum("crh,hd->crd", attended, w_out, preferred_element_type=jnp.float32).astype(
            jnp.bfloat16
        ),
        "head",
        scatter_dimension=0,
        tiled=True,
    ).astype(jnp.float32)
    context = (values + jnp.transpose(mixed, (1, 0, 2))).astype(jnp.bfloat16)
    padded = with_halo(context, (("tile", 0), ("head", 1)), 1).astype(jnp.float32)
    conv = jnp.zeros((rows, cols_dev, width), jnp.float32)
    for i in range(3):
        for j in range(3):
            conv = conv + padded[i : i + rows, j : j + cols_dev] * dw_weight[i, j]
    hidden = jax.nn.gelu(conv + join_bias).astype(jnp.bfloat16)
    projected_out = jnp.einsum("rcd,de->rce", hidden, w_join, preferred_element_type=jnp.float32)
    return (context.astype(jnp.float32) + projected_out).astype(jnp.bfloat16)


MESH = pl.DeviceIdType.MESH


def fused_kernel(
    tiles,
    parts,
    bott_ref,
    gain_ref,
    wqkv_hbm,
    wout_hbm,
    dw_ref,
    bias_ref,
    wjoin_hbm,
    out_ref,
    wqkv,
    wout,
    wjoin,
    nrm,
    snd,
    rcv,
    asnd,
    arcv,
    psnd,
    prcv,
    pad,
    hrow_s,
    hcol_s,
    hrow,
    hcol,
    wsem,
    nsend,
    nrecv,
    qsend,
    qrecv,
    asend,
    arecv,
    psend,
    precv,
    hsend,
    hrecv,
):
    f32, bf16 = jnp.float32, jnp.bfloat16
    t = lax.axis_index("tile")
    z = lax.axis_index("head")
    rows, cols, width = bott_ref.shape
    tok = rows * cols
    local = wqkv.shape[2]
    heads = tiles // parts
    head_dim = local // heads
    qpart = tok // parts
    z0, z1 = lax.rem(z, 2), z // 2

    def zpeer(k):
        return lax.rem(z0 + k % 2, 2) + 2 * lax.rem(z1 + k // 2, 2)

    zleft, zright = lax.rem(z + 3, 4), lax.rem(z + 1, 4)
    tup, tdown = lax.rem(t + tiles - 1, tiles), lax.rem(t + 1, tiles)

    loads = [
        pltpu.make_async_copy(wqkv_hbm, wqkv, wsem.at[0]),
        pltpu.make_async_copy(wout_hbm, wout, wsem.at[1]),
        pltpu.make_async_copy(wjoin_hbm, wjoin, wsem.at[2]),
    ]
    for load in loads:
        load.start()

    barrier = pltpu.get_barrier_semaphore()
    for k in range(1, 4):
        pl.semaphore_signal(barrier, inc=1, device_id=(t, zpeer(k)), device_id_type=MESH)

    @pl.loop(1, tiles)
    def _(p):
        pl.semaphore_signal(
            barrier, inc=1, device_id=(lax.rem(t + p, tiles), z), device_id_type=MESH
        )

    for dt in (tup, tdown):
        for dz in (zleft, zright):
            pl.semaphore_signal(barrier, inc=1, device_id=(dt, dz), device_id_type=MESH)

    values = bott_ref[...].reshape(tok, width).astype(f32)
    mean = jnp.mean(values * values, axis=-1, keepdims=True)
    nrm[0] = (values * lax.rsqrt(mean + 1e-06) * gain_ref[...]).astype(bf16)
    pad[...] = jnp.zeros_like(pad)

    pl.semaphore_wait(barrier, 3 + (tiles - 1) + 4)

    ncopies = []
    for k in (1, 2, 3):
        copy = pltpu.make_async_remote_copy(
            src_ref=nrm.at[0],
            dst_ref=nrm.at[k],
            send_sem=nsend.at[k - 1],
            recv_sem=nrecv.at[k - 1],
            device_id=(t, zpeer(k)),
            device_id_type=MESH,
        )
        copy.start()
        ncopies.append(copy)
    loads[0].wait()

    low = lax.broadcasted_iota(jnp.int32, (tok, 2 * head_dim), 1) < head_dim
    zero = jnp.zeros((tok, 2 * head_dim), f32)
    lanes = 2 * head_dim
    scale = 1.0 / head_dim**0.5

    def all_of(ref, sem):
        pltpu.make_async_copy(ref, ref, sem).wait()

    for k in range(4):
        if k > 0:
            ncopies[k - 1].wait_recv()
        x = nrm[k]
        q = jnp.dot(x, wqkv[0], preferred_element_type=f32) * scale
        key = jnp.dot(x, wqkv[1], preferred_element_type=f32)
        val = jnp.dot(x, wqkv[2], preferred_element_type=f32)
        for pair in range(heads // 2):
            cut = slice(pair * lanes, (pair + 1) * lanes)
            v2 = val[:, cut]
            k2 = pltpu.roll(key[:, cut], head_dim, 1)
            q2 = pltpu.roll(q[:, cut], head_dim, 1)
            even = jnp.where(low, v2, k2).astype(bf16)
            odd = jnp.where(low, k2, v2).astype(bf16)
            qeven = jnp.where(low, zero, q2).astype(bf16)
            qodd = jnp.where(low, q2, zero).astype(bf16)
            for h, kv, qq in ((2 * pair, even, qeven), (2 * pair + 1, odd, qodd)):
                for c in range(parts):
                    d = h * parts + c
                    snd[k, d, :tok] = kv
                    snd[k, d, tok:] = qq[c * qpart : (c + 1) * qpart]

        @pl.loop(1, tiles)
        def _(p):
            j = lax.rem(t + p, tiles)
            pltpu.make_async_remote_copy(
                src_ref=snd.at[k, j],
                dst_ref=rcv.at[k, t],
                send_sem=qsend.at[k],
                recv_sem=qrecv.at[k],
                device_id=(j, z),
                device_id_type=MESH,
            ).start()

        rcv[k, t] = snd[k, t]

    for k in range(4):
        all_of(rcv.at[k, pl.ds(0, tiles - 1)], qrecv.at[k])

    loads[1].wait()
    order = (3, 2, 1, 0)
    kvs = [rcv[k, :, :tok].reshape(tiles * tok, lanes) for k in range(4)]
    own = [None]

    def project(k):
        all_of(arcv.at[k, pl.ds(0, tiles - 1)], arecv.at[k])
        lowb = lax.broadcasted_iota(jnp.int32, (tok, lanes), 1) < head_dim
        pieces = []
        for pair in range(heads // 2):
            first = arcv[k, 2 * pair * parts : (2 * pair + 1) * parts].reshape(tok, lanes)
            second = arcv[k, (2 * pair + 1) * parts : (2 * pair + 2) * parts].reshape(tok, lanes)
            pieces.append(jnp.where(lowb, first, second))
        mixed = jnp.dot(jnp.concatenate(pieces, axis=1), wout[...], preferred_element_type=f32)
        if k == 0:
            own[0] = mixed
            return None
        psnd[k - 1] = mixed.astype(bf16)
        copy = pltpu.make_async_remote_copy(
            src_ref=psnd.at[k - 1],
            dst_ref=prcv.at[k - 1],
            send_sem=psend.at[k - 1],
            recv_sem=precv.at[k - 1],
            device_id=(t, zpeer(k)),
            device_id_type=MESH,
        )
        copy.start()
        return copy

    pcopies = []
    for step, k in enumerate(order):
        qs = rcv[k, :, tok:].reshape(tiles * qpart, lanes)
        scores = [
            lax.dot_general(qs, kv, (((1,), (1,)), ((), ())), preferred_element_type=f32)
            for kv in kvs
        ]
        top = functools.reduce(jnp.maximum, [jnp.max(s, axis=-1, keepdims=True) for s in scores])
        total, summed = 0.0, 0.0
        for s, kv in zip(scores, kvs):
            w = jnp.exp(s - top)
            total = total + jnp.sum(w, axis=-1, keepdims=True)
            summed = summed + jnp.dot(w.astype(bf16), kv, preferred_element_type=f32)
        asnd[k] = (summed / total).astype(bf16).reshape(tiles, qpart, lanes)

        @pl.loop(1, tiles)
        def _(p):
            j = lax.rem(t + p, tiles)
            pltpu.make_async_remote_copy(
                src_ref=asnd.at[k, j],
                dst_ref=arcv.at[k, t],
                send_sem=asend.at[k],
                recv_sem=arecv.at[k],
                device_id=(j, z),
                device_id_type=MESH,
            ).start()

        arcv[k, t] = asnd[k, t]
        if step > 0:
            pcopies.append(project(order[step - 1]))
    project(order[-1])

    context = bott_ref[...].reshape(tok, width).astype(f32)
    mixed = own[0]
    for copy, k in zip(pcopies, order):
        copy.wait_recv()
        mixed = mixed + prcv[k - 1].astype(f32)
    context = (context + mixed).astype(bf16)
    wide = context.astype(f32).reshape(rows, cols, width)
    narrow = context.reshape(rows, cols, width)
    pad[1 : rows + 1, 8 : 8 + cols] = wide
    hrow_s[0] = narrow[0]
    hrow_s[1] = narrow[rows - 1]
    first_row = lax.broadcasted_iota(jnp.int32, (16, width), 0) == 0
    for side, c in ((0, 0), (1, cols - 1)):
        hcol_s[side] = jnp.where(
            first_row, wide[0, c : c + 1], wide[rows - 1, c : c + 1]
        ).astype(bf16)

    hcopies = []
    plan = [
        (hrow_s.at[1], hrow.at[0], (tdown, z)),
        (hrow_s.at[0], hrow.at[1], (tup, z)),
        (hcol_s.at[1], hcol.at[0], (t, zright)),
        (hcol_s.at[0], hcol.at[1], (t, zleft)),
        (hcol_s.at[1], hcol.at[2], (tdown, zright)),
        (hcol_s.at[0], hcol.at[3], (tdown, zleft)),
        (hcol_s.at[1], hcol.at[4], (tup, zright)),
        (hcol_s.at[0], hcol.at[5], (tup, zleft)),
    ]
    for n, (src, dst, target) in enumerate(plan):
        copy = pltpu.make_async_remote_copy(
            src_ref=src,
            dst_ref=dst,
            send_sem=hsend.at[n],
            recv_sem=hrecv.at[n],
            device_id=target,
            device_id_type=MESH,
        )
        copy.start()
        hcopies.append(copy)
    loads[2].wait()

    for copy in ncopies:
        copy.wait_send()
    for k in range(4):
        all_of(snd.at[k, pl.ds(0, tiles - 1)], qsend.at[k])
        all_of(asnd.at[k, pl.ds(0, tiles - 1)], asend.at[k])
    for copy in pcopies:
        copy.wait_send()

    for copy in hcopies:
        copy.wait_recv()
    up_ok = (t > 0).astype(f32)
    down_ok = (t < tiles - 1).astype(f32)
    left_ok = (z > 0).astype(f32)
    right_ok = (z < 3).astype(f32)
    end = 8 + cols
    pad[0, 8:end] = hrow[0].astype(f32) * up_ok
    pad[rows + 1, 8:end] = hrow[1].astype(f32) * down_ok
    for n, ok, at in ((0, left_ok, 7), (1, right_ok, end)):
        column = hcol[n].astype(f32) * ok
        pad[1, at : at + 1] = column[0:1]
        pad[2, at : at + 1] = column[1:2]
        above = hcol[2 + n].astype(f32) * (ok * up_ok)
        pad[0, at : at + 1] = above[1:2]
        below = hcol[4 + n].astype(f32) * (ok * down_ok)
        pad[rows + 1, at : at + 1] = below[0:1]

    total = context.astype(f32)
    step = 256
    for c in range(0, width, step):
        cut = slice(c, c + step)
        conv = jnp.zeros((rows, cols, step), f32)
        for i in range(3):
            for j in range(3):
                conv = conv + pad[i : i + rows, 7 + j : 7 + j + cols, cut] * dw_ref[i, j : j + 1, cut]
        hidden = jax.nn.gelu(conv + bias_ref[:, cut]).astype(bf16).reshape(tok, step)
        total = total + jnp.dot(hidden, wjoin[cut, :], preferred_element_type=f32)
    out_ref[...] = total.astype(bf16).reshape(rows, cols, width)
    for copy in hcopies:
        copy.wait_send()


def fused(tiles, parts, bott, norm_gain, w_qkv, w_out, dw_weight, join_bias, w_join):
    rows, cols, width = bott.shape
    tok = rows * cols
    local = w_qkv.shape[2]
    lanes = 2 * local * parts // tiles
    qpart = tok // parts
    bf16 = jnp.bfloat16
    vmem = pl.BlockSpec(memory_space=pltpu.VMEM)
    hbm = pl.BlockSpec(memory_space=pl.ANY)
    dma = pltpu.SemaphoreType.DMA
    return pl.pallas_call(
        functools.partial(fused_kernel, tiles, parts),
        out_shape=jax.ShapeDtypeStruct(bott.shape, bf16),
        in_specs=[vmem, vmem, hbm, hbm, vmem, vmem, hbm],
        out_specs=vmem,
        scratch_shapes=[
            pltpu.VMEM(w_qkv.shape, bf16),
            pltpu.VMEM(w_out.shape, bf16),
            pltpu.VMEM(w_join.shape, bf16),
            pltpu.VMEM((4, tok, width), bf16),
            pltpu.VMEM((4, tiles, tok + qpart, lanes), bf16),
            pltpu.VMEM((4, tiles, tok + qpart, lanes), bf16),
            pltpu.VMEM((4, tiles, qpart, lanes), bf16),
            pltpu.VMEM((4, tiles, qpart, lanes), bf16),
            pltpu.VMEM((3, tok, width), bf16),
            pltpu.VMEM((3, tok, width), bf16),
            pltpu.VMEM((rows + 2, cols + 16, width), jnp.float32),
            pltpu.VMEM((2, cols, width), bf16),
            pltpu.VMEM((2, 16, width), bf16),
            pltpu.VMEM((2, cols, width), bf16),
            pltpu.VMEM((6, 16, width), bf16),
            dma((3,)),
            dma((3,)),
            dma((3,)),
            dma((4,)),
            dma((4,)),
            dma((4,)),
            dma((4,)),
            dma((3,)),
            dma((3,)),
            dma((8,)),
            dma((8,)),
        ],
        compiler_params=pltpu.CompilerParams(
            collective_id=0, has_side_effects=True, vmem_limit_bytes=48 * 2**20
        ),
        cost_estimate=pl.CostEstimate(
            flops=2 * 10**9, bytes_accessed=5 * 10**6, transcendentals=2 * 10**6
        ),
    )(
        bott,
        norm_gain.reshape(1, width),
        w_qkv,
        w_out,
        dw_weight,
        join_bias.reshape(1, width),
        w_join,
    )


def per_device_any(*args):
    bott, w_qkv = args[0], args[2]
    rows, cols, width = bott.shape
    tiles = lax.axis_size("tile")
    heads = w_qkv.shape[2] // (width // HEADS)
    parts = tiles // heads
    fits = (
        lax.axis_size("head") == 4
        and parts * heads == tiles
        and heads % 2 == 0
        and width == HEADS * 64
        and rows == 2
        and cols % 16 == 0
        and (rows * cols) % (16 * parts) == 0
    )
    return fused(tiles, parts, *args) if fits else per_device(*args)


def solution(mesh):
    placed = (P("tile", "head", None), P(), P(None, None, "head"), P("head", None), P(), P(), P())
    return jax.shard_map(
        per_device_any, mesh=mesh, in_specs=placed, out_specs=P("tile", "head", None), check_vma=False
    )
```

```python
import functools
import math

import jax
import jax.numpy as jnp
from jax import lax
from jax.experimental import pallas as pl
from jax.experimental.pallas import tpu as pltpu
from jax.sharding import PartitionSpec as P

HEADS = 16


def with_halo(x, sides, width):
    for axis, dim in sides:
        size, length = (lax.axis_size(axis), x.shape[dim])
        up = [(i, (i + 1) % size) for i in range(size - 1)]
        down = [(j, i) for i, j in up]
        last = lax.slice_in_dim(x, length - width, length, axis=dim)
        leading = lax.slice_in_dim(x, 0, width, axis=dim)
        before = lax.ppermute(last, axis, up)
        after = lax.ppermute(leading, axis, down)
        x = jnp.concatenate([before, x, after], axis=dim)
    return x


def fold_blocks(state, queries, key_piece, value_piece, scale):
    count, heads_here, head_dim = key_piece.shape
    block = math.gcd(count, 2048)
    key_blocks = key_piece.reshape(count // block, block, heads_here, head_dim)
    value_blocks = value_piece.reshape(count // block, block, heads_here, head_dim)

    def one_block(inner, pair):
        maxes, totals, summed = inner
        key_block, value_block = pair
        scores = (
            jnp.einsum("qhe,khe->hqk", queries, key_block, preferred_element_type=jnp.float32)
            * scale
        )
        new_max = jnp.maximum(maxes, jnp.max(scores, axis=-1))
        weights = jnp.exp(scores - new_max[..., None])
        decay = jnp.exp(maxes - new_max)
        totals = totals * decay + jnp.sum(weights, axis=-1)
        summed = summed * decay[..., None] + jnp.einsum(
            "hqk,khe->hqe",
            weights.astype(jnp.bfloat16),
            value_block,
            preferred_element_type=jnp.float32,
        )
        return ((new_max, totals, summed), None)

    return lax.scan(one_block, state, (key_blocks, value_blocks))[0]


def empty_state(heads_here, query_count, head_dim):
    return (
        jnp.full((heads_here, query_count), -1e30, jnp.float32),
        jnp.zeros((heads_here, query_count), jnp.float32),
        jnp.zeros((heads_here, query_count, head_dim), jnp.float32),
    )


def per_device(bott, norm_gain, w_qkv, w_out, dw_weight, join_bias, w_join):
    rows, cols_dev, width = bott.shape
    values = bott.astype(jnp.float32)
    normed = (
        values * lax.rsqrt(jnp.mean(values * values, axis=-1, keepdims=True) + 1e-06) * norm_gain
    ).astype(jnp.bfloat16)
    gathered = lax.all_gather(normed, "head", axis=1, tiled=True)
    columns = gathered.shape[1]
    local_width = w_qkv.shape[2]
    head_dim = width // HEADS
    local_heads = local_width // head_dim
    seq_local = columns * rows
    scale = 1.0 / head_dim**0.5
    tokens = jnp.transpose(gathered, (1, 0, 2)).reshape(seq_local, width)
    projected = jnp.einsum(
        "td,jde->jte", tokens, w_qkv, preferred_element_type=jnp.float32
    ).astype(jnp.bfloat16)
    queries = projected[0].reshape(seq_local, local_heads, head_dim)
    keys = projected[1]
    vals = projected[2]
    start_state = empty_state(local_heads, seq_local, head_dim)
    key_piece = lax.all_gather(keys, "tile", axis=0, tiled=True)
    value_piece = lax.all_gather(vals, "tile", axis=0, tiled=True)
    count = key_piece.shape[0]
    maxes, totals, summed = fold_blocks(
        start_state,
        queries,
        key_piece.reshape(count, local_heads, head_dim),
        value_piece.reshape(count, local_heads, head_dim),
        scale,
    )
    attended = (summed / totals[..., None]).astype(jnp.bfloat16)
    attended = jnp.transpose(attended, (1, 0, 2)).reshape(columns, rows, local_width)
    mixed = lax.psum_scatter(
        jnp.einsum("crh,hd->crd", attended, w_out, preferred_element_type=jnp.float32).astype(
            jnp.bfloat16
        ),
        "head",
        scatter_dimension=0,
        tiled=True,
    ).astype(jnp.float32)
    context = (values + jnp.transpose(mixed, (1, 0, 2))).astype(jnp.bfloat16)
    padded = with_halo(context, (("tile", 0), ("head", 1)), 1).astype(jnp.float32)
    conv = jnp.zeros((rows, cols_dev, width), jnp.float32)
    for i in range(3):
        for j in range(3):
            conv = conv + padded[i : i + rows, j : j + cols_dev] * dw_weight[i, j]
    hidden = jax.nn.gelu(conv + join_bias).astype(jnp.bfloat16)
    projected_out = jnp.einsum("rcd,de->rce", hidden, w_join, preferred_element_type=jnp.float32)
    return (context.astype(jnp.float32) + projected_out).astype(jnp.bfloat16)


MESH = pl.DeviceIdType.MESH


def fused_kernel(
    tiles,
    parts,
    bott_hbm,
    gain_hbm,
    wqkv_hbm,
    wout_hbm,
    dw_hbm,
    bias_hbm,
    wjoin_hbm,
    out_ref,
    bott_ref,
    gain_ref,
    dw_ref,
    bias_ref,
    wqkv,
    wout,
    wjoin,
    nrm,
    snd,
    rcv,
    asnd,
    arcv,
    psnd,
    prcv,
    pad,
    hrow_s,
    hcol_s,
    hcol_f,
    hrow,
    hcol,
    wsem,
    nsend,
    nrecv,
    qsend,
    qrecv,
    asend,
    arecv,
    psend,
    precv,
    hsend,
    hrecv,
):
    f32, bf16 = jnp.float32, jnp.bfloat16
    t = lax.axis_index("tile")
    z = lax.axis_index("head")
    rows, cols, width = bott_ref.shape
    tok = rows * cols
    local = wqkv.shape[2]
    heads = tiles // parts
    head_dim = local // heads
    qpart = tok // parts
    z0, z1 = lax.rem(z, 2), z // 2

    def zpeer(k):
        return lax.rem(z0 + k % 2, 2) + 2 * lax.rem(z1 + k // 2, 2)

    zleft, zright = lax.rem(z + 3, 4), lax.rem(z + 1, 4)
    tup, tdown = lax.rem(t + tiles - 1, tiles), lax.rem(t + 1, tiles)

    loads = [
        pltpu.make_async_copy(wqkv_hbm, wqkv, wsem.at[0]),
        pltpu.make_async_copy(wout_hbm, wout, wsem.at[1]),
        pltpu.make_async_copy(wjoin_hbm, wjoin, wsem.at[2]),
    ]
    small = [
        pltpu.make_async_copy(bott_hbm, bott_ref, wsem.at[3]),
        pltpu.make_async_copy(gain_hbm, gain_ref, wsem.at[4]),
        pltpu.make_async_copy(dw_hbm, dw_ref, wsem.at[5]),
        pltpu.make_async_copy(bias_hbm, bias_ref, wsem.at[6]),
    ]
    for load in small[:2]:
        load.start()

    barrier = pltpu.get_barrier_semaphore()
    for k in range(1, 4):
        pl.semaphore_signal(barrier, inc=1, device_id=(t, zpeer(k)), device_id_type=MESH)

    @pl.loop(1, tiles)
    def _(p):
        pl.semaphore_signal(
            barrier, inc=1, device_id=(lax.rem(t + p, tiles), z), device_id_type=MESH
        )

    for dt in (tup, tdown):
        for dz in (zleft, zright):
            pl.semaphore_signal(barrier, inc=1, device_id=(dt, dz), device_id_type=MESH)

    for load in loads + small[2:]:
        load.start()
    for load in small[:2]:
        load.wait()
    values = bott_ref[...].reshape(tok, width).astype(f32)
    mean = jnp.mean(values * values, axis=-1, keepdims=True)
    nrm[0] = (values * lax.rsqrt(mean + 1e-06) * gain_ref[...]).astype(bf16)
    pad[...] = jnp.zeros_like(pad)

    pl.semaphore_wait(barrier, 3 + (tiles - 1) + 4)

    half = tok // 2
    ncopies = {}

    def pass_block(src, dst, k, n, part):
        copy = pltpu.make_async_remote_copy(
            src_ref=nrm.at[src, part],
            dst_ref=nrm.at[dst, part],
            send_sem=nsend.at[n],
            recv_sem=nrecv.at[n],
            device_id=(t, zpeer(k)),
            device_id_type=MESH,
        )
        copy.start()
        ncopies[n] = copy

    halves = (pl.ds(0, half), pl.ds(half, half))
    for n in (0, 1):
        pass_block(0, 2, 2, n, halves[n])
    pass_block(0, 1, 1, 4, pl.ds(0, tok))
    loads[0].wait()

    low = lax.broadcasted_iota(jnp.int32, (tok, 2 * head_dim), 1) < head_dim
    zero = jnp.zeros((tok, 2 * head_dim), f32)
    lanes = 2 * head_dim
    scale = 1.0 / head_dim**0.5

    def all_of(ref, sem):
        pltpu.make_async_copy(ref, ref, sem).wait()

    for k in (0, 2, 1, 3):
        if k == 2:
            for n in (0, 1):
                ncopies[n].wait_recv()
                pass_block(2, 3, 1, 2 + n, halves[n])
        elif k == 1:
            ncopies[4].wait_recv()
        elif k == 3:
            for n in (2, 3):
                ncopies[n].wait_recv()
        x = nrm[k]
        q = jnp.dot(x, wqkv[0], preferred_element_type=f32) * scale
        key = jnp.dot(x, wqkv[1], preferred_element_type=f32)
        val = jnp.dot(x, wqkv[2], preferred_element_type=f32)
        for pair in range(heads // 2):
            cut = slice(pair * lanes, (pair + 1) * lanes)
            v2 = val[:, cut]
            k2 = pltpu.roll(key[:, cut], head_dim, 1)
            q2 = pltpu.roll(q[:, cut], head_dim, 1)
            even = jnp.where(low, v2, k2).astype(bf16)
            odd = jnp.where(low, k2, v2).astype(bf16)
            qeven = jnp.where(low, zero, q2).astype(bf16)
            qodd = jnp.where(low, q2, zero).astype(bf16)
            for h, kv, qq in ((2 * pair, even, qeven), (2 * pair + 1, odd, qodd)):
                for c in range(parts):
                    d = h * parts + c
                    snd[k, d, :tok] = kv
                    snd[k, d, tok:] = qq[c * qpart : (c + 1) * qpart]

        @pl.loop(1, tiles)
        def _(p):
            j = lax.rem(t + p, tiles)
            pltpu.make_async_remote_copy(
                src_ref=snd.at[k, j],
                dst_ref=rcv.at[k, t],
                send_sem=qsend.at[k],
                recv_sem=qrecv.at[k],
                device_id=(j, z),
                device_id_type=MESH,
            ).start()

        rcv[k, t] = snd[k, t]

    for k in range(4):
        all_of(rcv.at[k, pl.ds(0, tiles - 1)], qrecv.at[k])

    loads[1].wait()
    order = (3, 2, 1, 0)
    kvs = [rcv[k, :, :tok].reshape(tiles * tok, lanes) for k in range(4)]
    own = [None]

    def project(k):
        all_of(arcv.at[k, pl.ds(0, tiles - 1)], arecv.at[k])
        lowb = lax.broadcasted_iota(jnp.int32, (tok, lanes), 1) < head_dim
        pieces = []
        for pair in range(heads // 2):
            first = arcv[k, 2 * pair * parts : (2 * pair + 1) * parts].reshape(tok, lanes)
            second = arcv[k, (2 * pair + 1) * parts : (2 * pair + 2) * parts].reshape(tok, lanes)
            pieces.append(jnp.where(lowb, first, second))
        mixed = jnp.dot(jnp.concatenate(pieces, axis=1), wout[...], preferred_element_type=f32)
        if k == 0:
            own[0] = mixed
            return None
        psnd[k - 1] = mixed.astype(bf16)
        copy = pltpu.make_async_remote_copy(
            src_ref=psnd.at[k - 1],
            dst_ref=prcv.at[k - 1],
            send_sem=psend.at[k - 1],
            recv_sem=precv.at[k - 1],
            device_id=(t, zpeer(k)),
            device_id_type=MESH,
        )
        copy.start()
        return copy

    pcopies = []
    for step, k in enumerate(order):
        qs = rcv[k, :, tok:].reshape(tiles * qpart, lanes)
        scores = [
            lax.dot_general(qs, kv, (((1,), (1,)), ((), ())), preferred_element_type=f32)
            for kv in kvs
        ]
        top = functools.reduce(jnp.maximum, [jnp.max(s, axis=-1, keepdims=True) for s in scores])
        total, summed = 0.0, 0.0
        for s, kv in zip(scores, kvs):
            w = jnp.exp(s - top)
            total = total + jnp.sum(w, axis=-1, keepdims=True)
            summed = summed + jnp.dot(w.astype(bf16), kv, preferred_element_type=f32)
        asnd[k] = (summed / total).astype(bf16).reshape(tiles, qpart, lanes)

        @pl.loop(1, tiles)
        def _(p):
            j = lax.rem(t + p, tiles)
            pltpu.make_async_remote_copy(
                src_ref=asnd.at[k, j],
                dst_ref=arcv.at[k, t],
                send_sem=asend.at[k],
                recv_sem=arecv.at[k],
                device_id=(j, z),
                device_id_type=MESH,
            ).start()

        arcv[k, t] = asnd[k, t]
        if step > 0:
            pcopies.append(project(order[step - 1]))
    project(order[-1])

    context = bott_ref[...].reshape(tok, width).astype(f32)
    mixed = own[0]
    for copy, k in zip(pcopies, order):
        copy.wait_recv()
        mixed = mixed + prcv[k - 1].astype(f32)
    context = (context + mixed).astype(bf16)
    wide = context.astype(f32).reshape(rows, cols, width)
    narrow = context.reshape(rows, cols, width)
    pad[1 : rows + 1, 8 : 8 + cols] = wide
    hrow_s[0] = narrow[0]
    hrow_s[1] = narrow[rows - 1]
    strips = width // 128
    for side, c in ((0, 0), (1, cols - 1)):
        for r in range(rows):
            for n in range(strips):
                hcol_f[side, r * strips + n : r * strips + n + 1] = wide[
                    r, c : c + 1, n * 128 : (n + 1) * 128
                ]
        hcol_s[side] = hcol_f[side].astype(bf16)

    hcopies = []
    plan = [
        (hrow_s.at[1], hrow.at[0], (tdown, z)),
        (hrow_s.at[0], hrow.at[1], (tup, z)),
        (hcol_s.at[1], hcol.at[0], (t, zright)),
        (hcol_s.at[0], hcol.at[1], (t, zleft)),
        (hcol_s.at[1], hcol.at[2], (tdown, zright)),
        (hcol_s.at[0], hcol.at[3], (tdown, zleft)),
        (hcol_s.at[1], hcol.at[4], (tup, zright)),
        (hcol_s.at[0], hcol.at[5], (tup, zleft)),
    ]
    for n, (src, dst, target) in enumerate(plan):
        copy = pltpu.make_async_remote_copy(
            src_ref=src,
            dst_ref=dst,
            send_sem=hsend.at[n],
            recv_sem=hrecv.at[n],
            device_id=target,
            device_id_type=MESH,
        )
        copy.start()
        hcopies.append(copy)
    for load in [loads[2]] + small[2:]:
        load.wait()

    for copy in ncopies.values():
        copy.wait_send()
    for k in range(4):
        all_of(snd.at[k, pl.ds(0, tiles - 1)], qsend.at[k])
        all_of(asnd.at[k, pl.ds(0, tiles - 1)], asend.at[k])
    for copy in pcopies:
        copy.wait_send()

    for copy in hcopies:
        copy.wait_recv()
    up_ok = (t > 0).astype(f32)
    down_ok = (t < tiles - 1).astype(f32)
    left_ok = (z > 0).astype(f32)
    right_ok = (z < 3).astype(f32)
    end = 8 + cols
    pad[0, 8:end] = hrow[0].astype(f32) * up_ok
    pad[rows + 1, 8:end] = hrow[1].astype(f32) * down_ok
    for n, ok, at in ((0, left_ok, 7), (1, right_ok, end)):
        column = hcol[n].astype(f32) * ok
        above = hcol[2 + n].astype(f32) * (ok * up_ok)
        below = hcol[4 + n].astype(f32) * (ok * down_ok)
        for row, cells, r in ((1, column, 0), (2, column, 1), (0, above, 1), (3, below, 0)):
            for m in range(strips):
                pad[row, at : at + 1, m * 128 : (m + 1) * 128] = cells[
                    r * strips + m : r * strips + m + 1
                ]

    total = context.astype(f32)
    step = 256
    for c in range(0, width, step):
        cut = slice(c, c + step)
        conv = jnp.zeros((rows, cols, step), f32)
        for i in range(3):
            for j in range(3):
                conv = conv + pad[i : i + rows, 7 + j : 7 + j + cols, cut] * dw_ref[i, j : j + 1, cut]
        hidden = jax.nn.gelu(conv + bias_ref[:, cut]).astype(bf16).reshape(tok, step)
        total = total + jnp.dot(hidden, wjoin[cut, :], preferred_element_type=f32)
    out_ref[...] = total.astype(bf16).reshape(rows, cols, width)
    for copy in hcopies:
        copy.wait_send()


def fused(tiles, parts, bott, norm_gain, w_qkv, w_out, dw_weight, join_bias, w_join):
    rows, cols, width = bott.shape
    tok = rows * cols
    local = w_qkv.shape[2]
    lanes = 2 * local * parts // tiles
    qpart = tok // parts
    bf16 = jnp.bfloat16
    vmem = pl.BlockSpec(memory_space=pltpu.VMEM)
    hbm = pl.BlockSpec(memory_space=pltpu.HBM)
    dma = pltpu.SemaphoreType.DMA
    return pl.pallas_call(
        functools.partial(fused_kernel, tiles, parts),
        out_shape=jax.ShapeDtypeStruct(bott.shape, bf16),
        in_specs=[hbm] * 7,
        out_specs=vmem,
        scratch_shapes=[
            pltpu.VMEM(bott.shape, bf16),
            pltpu.VMEM((1, width), jnp.float32),
            pltpu.VMEM(dw_weight.shape, jnp.float32),
            pltpu.VMEM((1, width), jnp.float32),
            pltpu.VMEM(w_qkv.shape, bf16),
            pltpu.VMEM(w_out.shape, bf16),
            pltpu.VMEM(w_join.shape, bf16),
            pltpu.VMEM((4, tok, width), bf16),
            pltpu.VMEM((4, tiles, tok + qpart, lanes), bf16),
            pltpu.VMEM((4, tiles, tok + qpart, lanes), bf16),
            pltpu.VMEM((4, tiles, qpart, lanes), bf16),
            pltpu.VMEM((4, tiles, qpart, lanes), bf16),
            pltpu.VMEM((3, tok, width), bf16),
            pltpu.VMEM((3, tok, width), bf16),
            pltpu.VMEM((rows + 2, cols + 16, width), jnp.float32),
            pltpu.VMEM((2, cols, width), bf16),
            pltpu.VMEM((2, rows * width // 128, 128), bf16),
            pltpu.VMEM((2, rows * width // 128, 128), jnp.float32),
            pltpu.VMEM((2, cols, width), bf16),
            pltpu.VMEM((6, rows * width // 128, 128), bf16),
            dma((7,)),
            dma((5,)),
            dma((5,)),
            dma((4,)),
            dma((4,)),
            dma((4,)),
            dma((4,)),
            dma((3,)),
            dma((3,)),
            dma((8,)),
            dma((8,)),
        ],
        compiler_params=pltpu.CompilerParams(
            collective_id=0, has_side_effects=True, vmem_limit_bytes=56 * 2**20
        ),
        cost_estimate=pl.CostEstimate(
            flops=2 * 10**9, bytes_accessed=5 * 10**6, transcendentals=2 * 10**6
        ),
    )(
        bott,
        norm_gain.reshape(1, width),
        w_qkv,
        w_out,
        dw_weight,
        join_bias.reshape(1, width),
        w_join,
    )


def per_device_any(*args):
    bott, w_qkv = args[0], args[2]
    rows, cols, width = bott.shape
    tiles = lax.axis_size("tile")
    heads = w_qkv.shape[2] // (width // HEADS)
    parts = tiles // heads
    fits = (
        lax.axis_size("head") == 4
        and parts * heads == tiles
        and heads % 2 == 0
        and width == HEADS * 64
        and rows == 2
        and cols % 16 == 0
        and (rows * cols) % (16 * parts) == 0
    )
    return fused(tiles, parts, *args) if fits else per_device(*args)


def solution(mesh):
    placed = (P("tile", "head", None), P(), P(None, None, "head"), P("head", None), P(), P(), P())
    return jax.shard_map(
        per_device_any, mesh=mesh, in_specs=placed, out_specs=P("tile", "head", None), check_vma=False
    )
```

```python
import functools
import math

import jax
import jax.numpy as jnp
from jax import lax
from jax.experimental import pallas as pl
from jax.experimental.pallas import tpu as pltpu
from jax.sharding import PartitionSpec as P

HEADS = 16


def with_halo(x, sides, width):
    for axis, dim in sides:
        size, length = (lax.axis_size(axis), x.shape[dim])
        up = [(i, (i + 1) % size) for i in range(size - 1)]
        down = [(j, i) for i, j in up]
        last = lax.slice_in_dim(x, length - width, length, axis=dim)
        leading = lax.slice_in_dim(x, 0, width, axis=dim)
        before = lax.ppermute(last, axis, up)
        after = lax.ppermute(leading, axis, down)
        x = jnp.concatenate([before, x, after], axis=dim)
    return x


def fold_blocks(state, queries, key_piece, value_piece, scale):
    count, heads_here, head_dim = key_piece.shape
    block = math.gcd(count, 2048)
    key_blocks = key_piece.reshape(count // block, block, heads_here, head_dim)
    value_blocks = value_piece.reshape(count // block, block, heads_here, head_dim)

    def one_block(inner, pair):
        maxes, totals, summed = inner
        key_block, value_block = pair
        scores = (
            jnp.einsum("qhe,khe->hqk", queries, key_block, preferred_element_type=jnp.float32)
            * scale
        )
        new_max = jnp.maximum(maxes, jnp.max(scores, axis=-1))
        weights = jnp.exp(scores - new_max[..., None])
        decay = jnp.exp(maxes - new_max)
        totals = totals * decay + jnp.sum(weights, axis=-1)
        summed = summed * decay[..., None] + jnp.einsum(
            "hqk,khe->hqe",
            weights.astype(jnp.bfloat16),
            value_block,
            preferred_element_type=jnp.float32,
        )
        return ((new_max, totals, summed), None)

    return lax.scan(one_block, state, (key_blocks, value_blocks))[0]


def empty_state(heads_here, query_count, head_dim):
    return (
        jnp.full((heads_here, query_count), -1e30, jnp.float32),
        jnp.zeros((heads_here, query_count), jnp.float32),
        jnp.zeros((heads_here, query_count, head_dim), jnp.float32),
    )


def per_device(bott, norm_gain, w_qkv, w_out, dw_weight, join_bias, w_join):
    rows, cols_dev, width = bott.shape
    values = bott.astype(jnp.float32)
    normed = (
        values * lax.rsqrt(jnp.mean(values * values, axis=-1, keepdims=True) + 1e-06) * norm_gain
    ).astype(jnp.bfloat16)
    gathered = lax.all_gather(normed, "head", axis=1, tiled=True)
    columns = gathered.shape[1]
    local_width = w_qkv.shape[2]
    head_dim = width // HEADS
    local_heads = local_width // head_dim
    seq_local = columns * rows
    scale = 1.0 / head_dim**0.5
    tokens = jnp.transpose(gathered, (1, 0, 2)).reshape(seq_local, width)
    projected = jnp.einsum(
        "td,jde->jte", tokens, w_qkv, preferred_element_type=jnp.float32
    ).astype(jnp.bfloat16)
    queries = projected[0].reshape(seq_local, local_heads, head_dim)
    keys = projected[1]
    vals = projected[2]
    start_state = empty_state(local_heads, seq_local, head_dim)
    key_piece = lax.all_gather(keys, "tile", axis=0, tiled=True)
    value_piece = lax.all_gather(vals, "tile", axis=0, tiled=True)
    count = key_piece.shape[0]
    maxes, totals, summed = fold_blocks(
        start_state,
        queries,
        key_piece.reshape(count, local_heads, head_dim),
        value_piece.reshape(count, local_heads, head_dim),
        scale,
    )
    attended = (summed / totals[..., None]).astype(jnp.bfloat16)
    attended = jnp.transpose(attended, (1, 0, 2)).reshape(columns, rows, local_width)
    mixed = lax.psum_scatter(
        jnp.einsum("crh,hd->crd", attended, w_out, preferred_element_type=jnp.float32).astype(
            jnp.bfloat16
        ),
        "head",
        scatter_dimension=0,
        tiled=True,
    ).astype(jnp.float32)
    context = (values + jnp.transpose(mixed, (1, 0, 2))).astype(jnp.bfloat16)
    padded = with_halo(context, (("tile", 0), ("head", 1)), 1).astype(jnp.float32)
    conv = jnp.zeros((rows, cols_dev, width), jnp.float32)
    for i in range(3):
        for j in range(3):
            conv = conv + padded[i : i + rows, j : j + cols_dev] * dw_weight[i, j]
    hidden = jax.nn.gelu(conv + join_bias).astype(jnp.bfloat16)
    projected_out = jnp.einsum("rcd,de->rce", hidden, w_join, preferred_element_type=jnp.float32)
    return (context.astype(jnp.float32) + projected_out).astype(jnp.bfloat16)


MESH = pl.DeviceIdType.MESH


def fused_kernel(
    tiles,
    parts,
    bott_hbm,
    gain_hbm,
    wqkv_hbm,
    wout_hbm,
    dw_hbm,
    bias_hbm,
    wjoin_hbm,
    out_ref,
    bott_ref,
    gain_ref,
    dw_ref,
    bias_ref,
    wqkv,
    wout,
    wjoin,
    nrm,
    snd,
    rcv,
    asnd,
    arcv,
    psnd,
    prcv,
    pad,
    hrow_s,
    hcol_s,
    hcol_f,
    hrow,
    hcol,
    wsem,
    nsend,
    nrecv,
    qsend,
    qrecv,
    asend,
    arecv,
    psend,
    precv,
    hsend,
    hrecv,
):
    f32, bf16 = jnp.float32, jnp.bfloat16
    t = lax.axis_index("tile")
    z = lax.axis_index("head")
    rows, cols, width = bott_ref.shape
    tok = rows * cols
    local = wqkv.shape[2]
    heads = tiles // parts
    head_dim = local // heads
    qpart = tok // parts
    z0, z1 = lax.rem(z, 2), z // 2

    def zpeer(k):
        return lax.rem(z0 + k % 2, 2) + 2 * lax.rem(z1 + k // 2, 2)

    zleft, zright = lax.rem(z + 3, 4), lax.rem(z + 1, 4)
    tup, tdown = lax.rem(t + tiles - 1, tiles), lax.rem(t + 1, tiles)

    loads = [
        pltpu.make_async_copy(wqkv_hbm, wqkv, wsem.at[0]),
        pltpu.make_async_copy(wout_hbm, wout, wsem.at[1]),
        pltpu.make_async_copy(wjoin_hbm, wjoin, wsem.at[2]),
    ]
    small = [
        pltpu.make_async_copy(bott_hbm, bott_ref, wsem.at[3]),
        pltpu.make_async_copy(gain_hbm, gain_ref, wsem.at[4]),
        pltpu.make_async_copy(dw_hbm, dw_ref, wsem.at[5]),
        pltpu.make_async_copy(bias_hbm, bias_ref, wsem.at[6]),
    ]
    for load in small[:2]:
        load.start()

    barrier = pltpu.get_barrier_semaphore()
    for k in range(1, 4):
        pl.semaphore_signal(barrier, inc=1, device_id=(t, zpeer(k)), device_id_type=MESH)

    @pl.loop(1, tiles)
    def _(p):
        pl.semaphore_signal(
            barrier, inc=1, device_id=(lax.rem(t + p, tiles), z), device_id_type=MESH
        )

    for dt in (tup, tdown):
        for dz in (zleft, zright):
            pl.semaphore_signal(barrier, inc=1, device_id=(dt, dz), device_id_type=MESH)

    for load in loads + small[2:]:
        load.start()
    for load in small[:2]:
        load.wait()
    values = bott_ref[...].reshape(tok, width).astype(f32)
    mean = jnp.mean(values * values, axis=-1, keepdims=True)
    nrm[0] = (values * lax.rsqrt(mean + 1e-06) * gain_ref[...]).astype(bf16)
    pad[...] = jnp.zeros_like(pad)

    pl.semaphore_wait(barrier, 3 + (tiles - 1) + 4)

    half = tok // 2
    ncopies = {}

    def pass_block(src, dst, k, n, part):
        copy = pltpu.make_async_remote_copy(
            src_ref=nrm.at[src, part],
            dst_ref=nrm.at[dst, part],
            send_sem=nsend.at[n],
            recv_sem=nrecv.at[n],
            device_id=(t, zpeer(k)),
            device_id_type=MESH,
        )
        copy.start()
        ncopies[n] = copy

    halves = (pl.ds(0, half), pl.ds(half, half))
    for n in (0, 1):
        pass_block(0, 2, 2, n, halves[n])
    pass_block(0, 1, 1, 4, pl.ds(0, tok))
    loads[0].wait()

    low = lax.broadcasted_iota(jnp.int32, (tok, 2 * head_dim), 1) < head_dim
    zero = jnp.zeros((tok, 2 * head_dim), f32)
    lanes = 2 * head_dim
    scale = 1.0 / head_dim**0.5

    def all_of(ref, sem):
        pltpu.make_async_copy(ref, ref, sem).wait()

    for k in (0, 2, 1, 3):
        if k == 2:
            for n in (0, 1):
                ncopies[n].wait_recv()
                pass_block(2, 3, 1, 2 + n, halves[n])
        elif k == 1:
            ncopies[4].wait_recv()
        elif k == 3:
            for n in (2, 3):
                ncopies[n].wait_recv()
        x = nrm[k]
        q = jnp.dot(x, wqkv[0], preferred_element_type=f32) * scale
        key = jnp.dot(x, wqkv[1], preferred_element_type=f32)
        val = jnp.dot(x, wqkv[2], preferred_element_type=f32)
        for pair in range(heads // 2):
            cut = slice(pair * lanes, (pair + 1) * lanes)
            v2 = val[:, cut]
            k2 = pltpu.roll(key[:, cut], head_dim, 1)
            q2 = pltpu.roll(q[:, cut], head_dim, 1)
            even = jnp.where(low, v2, k2).astype(bf16)
            odd = jnp.where(low, k2, v2).astype(bf16)
            qeven = jnp.where(low, zero, q2).astype(bf16)
            qodd = jnp.where(low, q2, zero).astype(bf16)
            for h, kv, qq in ((2 * pair, even, qeven), (2 * pair + 1, odd, qodd)):
                for c in range(parts):
                    d = h * parts + c
                    snd[k, d, :tok] = kv
                    snd[k, d, tok:] = qq[c * qpart : (c + 1) * qpart]

        @pl.loop(1, tiles)
        def _(p):
            j = lax.rem(t + p, tiles)
            pltpu.make_async_remote_copy(
                src_ref=snd.at[k, j],
                dst_ref=rcv.at[k, t],
                send_sem=qsend.at[k],
                recv_sem=qrecv.at[k],
                device_id=(j, z),
                device_id_type=MESH,
            ).start()

        rcv[k, t] = snd[k, t]

    loads[1].wait()
    order = (2, 3, 1, 0)
    kvs = []
    own = [None]

    def project(k):
        all_of(arcv.at[k, pl.ds(0, tiles - 1)], arecv.at[k])
        lowb = lax.broadcasted_iota(jnp.int32, (tok, lanes), 1) < head_dim
        pieces = []
        for pair in range(heads // 2):
            first = arcv[k, 2 * pair * parts : (2 * pair + 1) * parts].reshape(tok, lanes)
            second = arcv[k, (2 * pair + 1) * parts : (2 * pair + 2) * parts].reshape(tok, lanes)
            pieces.append(jnp.where(lowb, first, second))
        mixed = jnp.dot(jnp.concatenate(pieces, axis=1), wout[...], preferred_element_type=f32)
        if k == 0:
            own[0] = mixed
            return None
        psnd[k - 1] = mixed.astype(bf16)
        copy = pltpu.make_async_remote_copy(
            src_ref=psnd.at[k - 1],
            dst_ref=prcv.at[k - 1],
            send_sem=psend.at[k - 1],
            recv_sem=precv.at[k - 1],
            device_id=(t, zpeer(k)),
            device_id_type=MESH,
        )
        copy.start()
        return copy

    pcopies = []
    for step, k in enumerate(order):
        if step == 0:
            for n in (0, 2):
                all_of(rcv.at[n, pl.ds(0, tiles - 1)], qrecv.at[n])
        qs = rcv[k, :, tok:].reshape(tiles * qpart, lanes)
        scores = []
        for i, n in enumerate((0, 2, 1, 3)):
            if step == 0:
                if i > 1:
                    all_of(rcv.at[n, pl.ds(0, tiles - 1)], qrecv.at[n])
                kvs.append(rcv[n, :, :tok].reshape(tiles * tok, lanes))
            scores.append(
                lax.dot_general(
                    qs, kvs[i], (((1,), (1,)), ((), ())), preferred_element_type=f32
                )
            )
        top = functools.reduce(jnp.maximum, [jnp.max(s, axis=-1, keepdims=True) for s in scores])
        total, summed = 0.0, 0.0
        for s, kv in zip(scores, kvs):
            w = jnp.exp(s - top)
            total = total + jnp.sum(w, axis=-1, keepdims=True)
            summed = summed + jnp.dot(w.astype(bf16), kv, preferred_element_type=f32)
        asnd[k] = (summed / total).astype(bf16).reshape(tiles, qpart, lanes)

        @pl.loop(1, tiles)
        def _(p):
            j = lax.rem(t + p, tiles)
            pltpu.make_async_remote_copy(
                src_ref=asnd.at[k, j],
                dst_ref=arcv.at[k, t],
                send_sem=asend.at[k],
                recv_sem=arecv.at[k],
                device_id=(j, z),
                device_id_type=MESH,
            ).start()

        arcv[k, t] = asnd[k, t]
        if step > 0:
            pcopies.append(project(order[step - 1]))
    project(order[-1])

    context = bott_ref[...].reshape(tok, width).astype(f32)
    mixed = own[0]
    for copy, k in zip(pcopies, order):
        copy.wait_recv()
        mixed = mixed + prcv[k - 1].astype(f32)
    context = (context + mixed).astype(bf16)
    wide = context.astype(f32).reshape(rows, cols, width)
    narrow = context.reshape(rows, cols, width)
    pad[1 : rows + 1, 8 : 8 + cols] = wide
    hrow_s[0] = narrow[0]
    hrow_s[1] = narrow[rows - 1]
    strips = width // 128
    for side, c in ((0, 0), (1, cols - 1)):
        for r in range(rows):
            for n in range(strips):
                hcol_f[side, r * strips + n : r * strips + n + 1] = wide[
                    r, c : c + 1, n * 128 : (n + 1) * 128
                ]
        hcol_s[side] = hcol_f[side].astype(bf16)

    hcopies = []
    plan = [
        (hrow_s.at[1], hrow.at[0], (tdown, z)),
        (hrow_s.at[0], hrow.at[1], (tup, z)),
        (hcol_s.at[1], hcol.at[0], (t, zright)),
        (hcol_s.at[0], hcol.at[1], (t, zleft)),
        (hcol_s.at[1], hcol.at[2], (tdown, zright)),
        (hcol_s.at[0], hcol.at[3], (tdown, zleft)),
        (hcol_s.at[1], hcol.at[4], (tup, zright)),
        (hcol_s.at[0], hcol.at[5], (tup, zleft)),
    ]
    for n, (src, dst, target) in enumerate(plan):
        copy = pltpu.make_async_remote_copy(
            src_ref=src,
            dst_ref=dst,
            send_sem=hsend.at[n],
            recv_sem=hrecv.at[n],
            device_id=target,
            device_id_type=MESH,
        )
        copy.start()
        hcopies.append(copy)
    for load in [loads[2]] + small[2:]:
        load.wait()

    for copy in ncopies.values():
        copy.wait_send()
    for k in range(4):
        all_of(snd.at[k, pl.ds(0, tiles - 1)], qsend.at[k])
        all_of(asnd.at[k, pl.ds(0, tiles - 1)], asend.at[k])
    for copy in pcopies:
        copy.wait_send()

    for copy in hcopies:
        copy.wait_recv()
    up_ok = (t > 0).astype(f32)
    down_ok = (t < tiles - 1).astype(f32)
    left_ok = (z > 0).astype(f32)
    right_ok = (z < 3).astype(f32)
    end = 8 + cols
    pad[0, 8:end] = hrow[0].astype(f32) * up_ok
    pad[rows + 1, 8:end] = hrow[1].astype(f32) * down_ok
    for n, ok, at in ((0, left_ok, 7), (1, right_ok, end)):
        column = hcol[n].astype(f32) * ok
        above = hcol[2 + n].astype(f32) * (ok * up_ok)
        below = hcol[4 + n].astype(f32) * (ok * down_ok)
        for row, cells, r in ((1, column, 0), (2, column, 1), (0, above, 1), (3, below, 0)):
            for m in range(strips):
                pad[row, at : at + 1, m * 128 : (m + 1) * 128] = cells[
                    r * strips + m : r * strips + m + 1
                ]

    total = context.astype(f32)
    step = 256
    for c in range(0, width, step):
        cut = slice(c, c + step)
        conv = jnp.zeros((rows, cols, step), f32)
        for i in range(3):
            for j in range(3):
                conv = conv + pad[i : i + rows, 7 + j : 7 + j + cols, cut] * dw_ref[i, j : j + 1, cut]
        hidden = jax.nn.gelu(conv + bias_ref[:, cut]).astype(bf16).reshape(tok, step)
        total = total + jnp.dot(hidden, wjoin[cut, :], preferred_element_type=f32)
    out_ref[...] = total.astype(bf16).reshape(rows, cols, width)
    for copy in hcopies:
        copy.wait_send()


def fused(tiles, parts, bott, norm_gain, w_qkv, w_out, dw_weight, join_bias, w_join):
    rows, cols, width = bott.shape
    tok = rows * cols
    local = w_qkv.shape[2]
    lanes = 2 * local * parts // tiles
    qpart = tok // parts
    bf16 = jnp.bfloat16
    vmem = pl.BlockSpec(memory_space=pltpu.VMEM)
    hbm = pl.BlockSpec(memory_space=pltpu.HBM)
    dma = pltpu.SemaphoreType.DMA
    return pl.pallas_call(
        functools.partial(fused_kernel, tiles, parts),
        out_shape=jax.ShapeDtypeStruct(bott.shape, bf16),
        in_specs=[hbm] * 7,
        out_specs=vmem,
        scratch_shapes=[
            pltpu.VMEM(bott.shape, bf16),
            pltpu.VMEM((1, width), jnp.float32),
            pltpu.VMEM(dw_weight.shape, jnp.float32),
            pltpu.VMEM((1, width), jnp.float32),
            pltpu.VMEM(w_qkv.shape, bf16),
            pltpu.VMEM(w_out.shape, bf16),
            pltpu.VMEM(w_join.shape, bf16),
            pltpu.VMEM((4, tok, width), bf16),
            pltpu.VMEM((4, tiles, tok + qpart, lanes), bf16),
            pltpu.VMEM((4, tiles, tok + qpart, lanes), bf16),
            pltpu.VMEM((4, tiles, qpart, lanes), bf16),
            pltpu.VMEM((4, tiles, qpart, lanes), bf16),
            pltpu.VMEM((3, tok, width), bf16),
            pltpu.VMEM((3, tok, width), bf16),
            pltpu.VMEM((rows + 2, cols + 16, width), jnp.float32),
            pltpu.VMEM((2, cols, width), bf16),
            pltpu.VMEM((2, rows * width // 128, 128), bf16),
            pltpu.VMEM((2, rows * width // 128, 128), jnp.float32),
            pltpu.VMEM((2, cols, width), bf16),
            pltpu.VMEM((6, rows * width // 128, 128), bf16),
            dma((7,)),
            dma((5,)),
            dma((5,)),
            dma((4,)),
            dma((4,)),
            dma((4,)),
            dma((4,)),
            dma((3,)),
            dma((3,)),
            dma((8,)),
            dma((8,)),
        ],
        compiler_params=pltpu.CompilerParams(
            collective_id=0, has_side_effects=True, vmem_limit_bytes=56 * 2**20
        ),
        cost_estimate=pl.CostEstimate(
            flops=2 * 10**9, bytes_accessed=5 * 10**6, transcendentals=2 * 10**6
        ),
    )(
        bott,
        norm_gain.reshape(1, width),
        w_qkv,
        w_out,
        dw_weight,
        join_bias.reshape(1, width),
        w_join,
    )


def per_device_any(*args):
    bott, w_qkv = args[0], args[2]
    rows, cols, width = bott.shape
    tiles = lax.axis_size("tile")
    heads = w_qkv.shape[2] // (width // HEADS)
    parts = tiles // heads
    fits = (
        lax.axis_size("head") == 4
        and parts * heads == tiles
        and heads % 2 == 0
        and width == HEADS * 64
        and rows == 2
        and cols % 16 == 0
        and (rows * cols) % (16 * parts) == 0
    )
    return fused(tiles, parts, *args) if fits else per_device(*args)


def solution(mesh):
    placed = (P("tile", "head", None), P(), P(None, None, "head"), P("head", None), P(), P(), P())
    return jax.shard_map(
        per_device_any, mesh=mesh, in_specs=placed, out_specs=P("tile", "head", None), check_vma=False
    )
```
